128 devices in a mesh: comp: 2 (over core), tile: 64 (over x, y, z).
Axes of the slice: x: 4, y: 4, z: 4, core: 2. Of those that a mesh axis runs over, the one named last changes fastest.
Arguments:
- surface: float32 [2, 8, 8192, 128], P('comp', None, 'tile'), may hold values from -2.5 to 6, as said below
- area: float32 [2, 8192, 128], P('comp', 'tile'), may hold values from 0.25 to 9, as said below
- sea: int32 [8192, 128], P('tile'), may hold values 0 or 1
- weights: float32 [2, 16384, 128, 128], P('comp', 'tile'), may hold values from 0 to 0.015625
- src_row: int32 [2, 16384], P('comp', 'tile'), may hold values from 0 to 127
- dst_tile: int32 [2, 16384, 1], P('comp', 'tile'), may hold values from 0 to 63; in each aligned block of 256 rows (0 to 255, 256 to 511, ..., all dimensions but the last counted through in order) at most 8 rows name the same one
- dst_local: int32 [2, 16384], P('comp', 'tile'), may hold values from 0 to 127
Outputs:
- remapped: float32 [2, 8, 8192, 128], P('comp', None, 'tile')
The draws below stay inside these ranges and needn't reach their ends.
Inputs may be any that keep to these rules, and one draw needn't show every extreme that they name: `surface`: each component's fields, of order one with a mean for each field. `area`: positive cell areas. `dst_tile`: the weight blocks held by one tile aim at most 8 blocks at one target tile.
All inputs are finite; a program needn't handle non-finite values. No bound on the sum of `sea` on one device may be relied on, other than what follows from the above.
Results may differ from the reference program's by a relative error of at most 0.0001.
Values sent between devices are 32-bit elements; how exact they have to be, the bound alone decides.
No kernel may reach another device: no remote copies, remote signals or barrier semaphores. Data moves between devices by JAX's collectives and lax.ppermute only.
A program may use at most 64 MiB of HBM per device.

```python
import math
import jax
import jax.numpy as jnp
import numpy as np
from jax import lax

FIELDS = 8
CELLS = 128
ROWS_DEV = 128
ROWS = 8192
BLOCKS_DEV = 256
BLOCKS = 16384
SLOTS = 8
N_TILE = 64


def draw_surface(key, part):
    key = jax.random.fold_in(key, 1)
    key_mean, key_noise = jax.random.split(key, 2)
    field_means = jax.random.uniform(key_mean, (2, FIELDS, 1, 1), jnp.float32, 0.5, 2.0)
    roughness = jnp.clip(0.6 * jax.random.normal(key_noise, (2, FIELDS, ROWS, CELLS), jnp.float32), -2.4, 2.4)
    values = field_means + roughness
    return values.astype(jnp.float32)


def draw_area(key, part):
    key = jax.random.fold_in(key, 2)
    rising = 1.0 + 2.0 * jnp.arange(ROWS, dtype=jnp.float32)[None, :, None] / (ROWS - 1)
    across = 0.5 + jnp.arange(CELLS, dtype=jnp.float32)[None, None, :] / (CELLS - 1)
    variation = jnp.exp(jax.random.uniform(key, (2, ROWS, CELLS), jnp.float32, jnp.log(0.5), jnp.log(2.0)))
    return (rising * across * variation).astype(jnp.float32)


def draw_weights(key, part):
    key = jax.random.fold_in(key, 3)
    target_ramp = 0.3 + 0.7 * jnp.arange(CELLS, dtype=jnp.float32)[:, None] / (CELLS - 1)
    values = jax.random.uniform(key, (2, BLOCKS, CELLS, CELLS), jnp.float32, 0.0, 2.0 / CELLS)
    return (values * target_ramp).astype(jnp.float32)


def place_ends(entries, own_key, low, top_value):
    extent = entries.shape
    index_at = [jax.random.randint(jax.random.fold_in(own_key, axis), (), 0, extent[axis]) for axis in range(len(extent))]
    entries = entries.at[tuple(index_at)].set(low)
    longest = extent.index(max(extent))
    index_at[longest] = (index_at[longest] + 1) % extent[longest]
    return entries.at[tuple(index_at)].set(top_value)


def deal_out(own_key, own, number, rows, number_of, top, reach, lean):
    sequence = jax.random.permutation(own_key, number_of)
    packed, usual = portions_of(number_of, rows * top, reach, lean, True), portions_of(number_of, rows * top, reach, lean, False)
    places = jnp.arange(number_of)

    def named(sizes, offset_by):
        used = int((sizes > 0).sum())
        fixed = max(1, used // 4)
        moved = fixed + (places - fixed + offset_by * (used - fixed)) % max(1, number_of - fixed)
        return jnp.zeros((number_of,), jnp.int32).at[sequence[jnp.where(places < fixed, places, moved)]].set(jnp.asarray(sizes, jnp.int32))

    sizes = jnp.where(number % 4 == 0, named(packed, number // 4), named(usual, number - number // 4 - 1))
    mixed = jax.random.permutation(jax.random.fold_in(own, 3), number_of)
    source_of, taker = mixed[0:number_of // 2 * 2:2], mixed[1:number_of // 2 * 2:2]
    slack = jnp.minimum(sizes[source_of] - 1, reach - sizes[taker]) // 2
    slack = jnp.where((source_of == sequence[0]) | (taker == sequence[0]) | (sizes[taker] == 0), 0, jnp.maximum(slack, 0))
    moved = jax.random.randint(jax.random.fold_in(own, 4), (number_of // 2,), 0, 1 << 20) % (slack + 1)
    sizes = sizes.at[source_of].add(-moved).at[taker].add(moved)
    members = jnp.searchsorted(jnp.cumsum(sizes), jnp.arange(rows * top), side="right").astype(jnp.int32)
    grid = members.reshape(top, rows).T
    grid = grid[jax.random.permutation(jax.random.fold_in(own, 1), rows)]
    offset_by = jax.random.randint(jax.random.fold_in(own, 2), (rows, 1), 0, top)
    return jnp.take_along_axis(grid, (jnp.arange(top)[None, :] + offset_by) % top, axis=1)


def portions_of(count, total, limit, lean, full):
    portions = [(1 << 20) // math.isqrt(standing ** lean) + 1 for standing in range(1, count + 1)]
    largest = limit if full else min(limit, max(-(-total // count), total * portions[0] // sum(portions)))
    least = 1 if total - largest >= count - 1 else 0
    holding, surplus = [largest] + [least] * (count - 1), total - largest - least * (count - 1)
    while surplus > 0:
        movable = [i for i in range(1, count) if holding[i] < largest] or [i for i in range(1, count) if holding[i] < limit]
        pool, budget = sum([portions[i] for i in movable]), surplus
        for i in movable:
            extra = min(limit - holding[i], max(1, budget * portions[i] // pool), surplus)
            holding[i] = holding[i] + extra
            surplus = surplus - extra
    return np.array(holding)


def setup_inputs(seed: int = 0) -> dict:
    key_of = jax.random.split(jax.random.key(seed), 8)
    surface = draw_surface(jax.random.fold_in(key_of[7], 71), 0)
    area = draw_area(jax.random.fold_in(key_of[7], 71), 0)
    sea = place_ends((jax.random.randint(key_of[2], (ROWS, CELLS), 0, 10) < 7).astype(jnp.int32), jax.random.fold_in(key_of[2], 1), 0, 1)
    weights = draw_weights(jax.random.fold_in(key_of[7], 71), 0)
    src_row = place_ends(jax.random.randint(key_of[4], (2, BLOCKS), 0, ROWS_DEV), jax.random.fold_in(key_of[4], 1), 0, ROWS_DEV - 1).astype(jnp.int32)
    dst_tile_keys = jax.random.split(jax.random.fold_in(key_of[5], 1), 2 * BLOCKS // BLOCKS_DEV)
    dst_tile_turns = jax.random.permutation(jax.random.fold_in(key_of[5], 3), 2 * BLOCKS // BLOCKS_DEV)
    dst_tile = jax.vmap(lambda own, number: deal_out(jax.random.fold_in(key_of[5], 2), own, number, BLOCKS_DEV, N_TILE, 1, SLOTS, 2))(dst_tile_keys, dst_tile_turns).reshape((2, BLOCKS, 1))
    dst_local = place_ends(jax.random.randint(key_of[6], (2, BLOCKS), 0, ROWS_DEV), jax.random.fold_in(key_of[6], 1), 0, ROWS_DEV - 1).astype(jnp.int32)
    return dict(surface=surface, area=area, sea=sea, weights=weights, src_row=src_row, dst_tile=dst_tile, dst_local=dst_local)


smooth_rate = 0.2


def smooth_side(values):
    padded = jnp.pad(values, ((0, 0), (1, 1), (1, 1)))
    beside_all = padded[:, :-2, 1:-1] + padded[:, 2:, 1:-1] + padded[:, 1:-1, :-2] + padded[:, 1:-1, 2:]
    return values + smooth_rate * (beside_all - 4.0 * values)


def reference(surface, area, sea, weights, src_row, dst_tile, dst_local):
    owner_tile = jnp.arange(BLOCKS, dtype=jnp.int32) // BLOCKS_DEV
    sea_float = sea.astype(jnp.float32)
    side_masks = jnp.stack([jnp.ones_like(sea_float), sea_float])
    smoothed = jnp.stack([smooth_side(surface[0]), smooth_side(surface[1])])
    source_total = jnp.sum(area[:, None] * smoothed, axis=(2, 3))
    remapped_list = []
    for section in range(2):
        source_index = (owner_tile * ROWS_DEV + src_row[section]).astype(jnp.int32)
        picked = smoothed[section][:, source_index, :]
        products = jnp.einsum("fkc,kdc->kfd", picked, weights[section], precision=lax.Precision.HIGHEST)
        target = (dst_tile[section, :, 0] * ROWS_DEV + dst_local[section]).astype(jnp.int32)
        summed = jnp.zeros((ROWS, FIELDS, CELLS), jnp.float32).at[target].add(products)
        remapped_list.append(jnp.transpose(summed, (1, 0, 2)))
    received = jnp.stack([remapped_list[1], remapped_list[0]])
    masked = received * side_masks[:, None]
    target_total = jnp.sum(area[:, None] * masked, axis=(2, 3))
    target_area = jnp.sum(area * side_masks, axis=(1, 2))
    opposite = source_total[::-1]
    deficit = (opposite - target_total) / target_area[:, None]
    return masked + side_masks[:, None] * deficit[:, :, None, None]
```

```python
import functools

import jax
import jax.numpy as jnp
from jax import lax
from jax.experimental import pallas as pl
from jax.experimental.pallas import tpu as pltpu
from jax.sharding import PartitionSpec as P

RATE = 0.2
LANES = 128
SUB = 8
CHUNKS = 16
EDGES = 16

F32 = jnp.float32
BF16 = jnp.bfloat16
I32 = jnp.int32


def split_rows(rows):
    lead = rows.astype(BF16).astype(F32)
    return jnp.concatenate([lead, rows - lead], axis=0).astype(BF16)


def block_product(rows2, w):
    lead = w.astype(BF16)
    rest = (w - lead.astype(F32)).astype(BF16)
    dims = (((1,), (1,)), ((), ()))
    a = lax.dot_general(rows2, lead, dims, preferred_element_type=F32)
    b = lax.dot_general(rows2, rest, dims, preferred_element_type=F32)
    t = a + b
    return t[:SUB] + t[SUB:]


def products_kernel(
    row_ref, surf_ref, area_ref, w_ref,
    prod_ref, part_ref, edge_w_ref, edge_ref,
    wbuf, smooth, rows2, sems, *, blocks, fields, rows,
):
    per = blocks // CHUNKS

    def fetch(c):
        span = pl.ds(c * per, per)
        return pltpu.make_async_copy(w_ref.at[0, span], wbuf.at[span], sems.at[c])

    for c in range(CHUNKS):
        fetch(c).start()

    r_iota = lax.broadcasted_iota(I32, (rows, LANES), 0)
    c_iota = lax.broadcasted_iota(I32, (rows, LANES), 1)
    area = area_ref[0]
    for f in range(fields):
        s = surf_ref[0, f]
        n = jnp.where(r_iota > 0, pltpu.roll(s, 1, 0), 0.0)
        n += jnp.where(r_iota < rows - 1, pltpu.roll(s, rows - 1, 0), 0.0)
        n += jnp.where(c_iota > 0, pltpu.roll(s, 1, 1), 0.0)
        n += jnp.where(c_iota < LANES - 1, pltpu.roll(s, LANES - 1, 1), 0.0)
        sm = s + RATE * (n - 4.0 * s)
        part_ref[pl.ds(f, 1), :] = jnp.sum(area * sm, axis=0, keepdims=True)
        smooth[pl.ds(f, rows, stride=fields), :] = sm

    def halves(g, carry):
        rows2[g] = split_rows(smooth[pl.ds(pl.multiple_of(g * SUB, SUB), SUB), :])
        return carry

    lax.fori_loop(0, rows, halves, 0, unroll=8)

    def chunk(c, n_edge):
        fetch(c).wait()
        for b in range(per):
            k = c * per + b
            g = row_ref[0, k]
            edge_ref[n_edge] = k
            n_edge += jnp.logical_or(g == 0, g == rows - 1).astype(I32)
            at = pl.multiple_of(k * SUB, SUB)
            prod_ref[pl.ds(at, SUB), :] = block_product(rows2[g], wbuf[k])
        return n_edge

    n_edge = lax.fori_loop(0, CHUNKS, chunk, 0)
    edge_ref[blocks] = n_edge

    def keep(e, carry):
        edge_w_ref[e] = wbuf[edge_ref[e]]
        return carry

    lax.fori_loop(0, jnp.minimum(n_edge, EDGES), keep, 0)


def pack_kernel(
    row_ref, tile_ref, local_ref, edge_ref, prod_ref, part_ref, edge_w_ref, before_ref, after_ref,
    area_ref, w_ref,
    packed_ref, total_ref, wbuf, count, place, sem, *, blocks, fields, rows, slots, tiles,
):
    pitch = (fields + 1) * slots

    def clear(t, carry):
        count[t] = 0
        base = pl.multiple_of(t * pitch + fields * slots, SUB)
        packed_ref[pl.ds(base, slots), :] = jnp.full((slots, LANES), -1.0, F32)
        return carry

    lax.fori_loop(0, tiles, clear, 0, unroll=8)

    def pack(k, carry):
        t = tile_ref[k]
        rank = count[t]
        count[t] = rank + 1
        at = t * pitch + rank
        place[k] = at
        packed_ref[pl.ds(at, fields, stride=slots), :] = prod_ref[pl.ds(pl.multiple_of(k * SUB, SUB), SUB), :]
        local = jnp.full((1, LANES), local_ref[0, k], I32)
        packed_ref[pl.ds(at + fields * slots, 1), :] = local.astype(F32)
        return carry

    lax.fori_loop(0, blocks, pack, 0, unroll=8)

    before = RATE * before_ref[...]
    after = RATE * after_ref[...]
    area = area_ref[0]
    total_ref[...] = part_ref[...] + area[0:1] * before + area[rows - 1 : rows] * after

    def add(e, w):
        k = edge_ref[e]
        halo = jnp.where(row_ref[0, k] == 0, before, after)
        spot = pl.ds(place[k], fields, stride=slots)
        packed_ref[spot, :] = packed_ref[spot, :] + block_product(split_rows(halo), w)

    def near(e, carry):
        add(e, edge_w_ref[e])
        return carry

    def far(e, carry):
        copy = pltpu.make_async_copy(w_ref.at[0, edge_ref[e]], wbuf, sem)
        copy.start()
        copy.wait()
        add(e, wbuf[...])
        return carry

    n_edge = edge_ref[blocks]
    lax.fori_loop(0, jnp.minimum(n_edge, EDGES), near, 0)
    lax.fori_loop(EDGES, n_edge, far, 0)


def place_kernel(
    section_ref, recv_ref, total_ref, area_ref, sea_ref, masked_ref, tail_ref,
    *, fields, rows, slots, tiles,
):
    count = tiles * slots
    target = recv_ref[:, fields * slots :, :].reshape(count, LANES)
    lane = lax.broadcasted_iota(I32, (count, rows), 1).astype(F32)
    placing = jnp.where(target == lane, 1.0, 0.0).T.astype(BF16)
    used = target >= 0.0
    first = section_ref[0] == 1
    mask = jnp.where(first, 1.0, sea_ref[...].astype(F32))
    weight = area_ref[0] * mask
    lane1 = lax.broadcasted_iota(I32, (1, LANES), 1)
    tail = jnp.where(lane1 == fields, jnp.sum(weight), 0.0)
    for f in range(fields):
        x = recv_ref[:, f * slots : (f + 1) * slots, :].reshape(count, LANES)
        x = jnp.where(used, x, 0.0)
        lead = x.astype(BF16)
        rest = (x - lead.astype(F32)).astype(BF16)
        got = jnp.dot(placing, lead, preferred_element_type=F32)
        got += jnp.dot(placing, rest, preferred_element_type=F32)
        masked_ref[f] = got * mask
        gap = jnp.sum(total_ref[pl.ds(f, 1), :]) - jnp.sum(weight * got)
        tail += jnp.where(lane1 == f, gap, 0.0)
    tail_ref[...] = jnp.broadcast_to(tail, (tiles, LANES))


def correct_kernel(section_ref, masked_ref, tail_ref, sea_ref, out_ref, *, fields):
    sums = jnp.sum(tail_ref[...], axis=0, keepdims=True)
    lane1 = lax.broadcasted_iota(I32, (1, LANES), 1)
    whole = jnp.sum(jnp.where(lane1 == fields, sums, 0.0), axis=1, keepdims=True)
    deficit = sums / whole
    first = section_ref[0] == 1
    mask = jnp.where(first, 1.0, sea_ref[...].astype(F32))
    for f in range(fields):
        d = jnp.sum(jnp.where(lane1 == f, deficit, 0.0), axis=1, keepdims=True)
        out_ref[0, f] = masked_ref[f] + mask * d


VMEM = pl.BlockSpec(memory_space=pltpu.VMEM)
SMEM = pl.BlockSpec(memory_space=pltpu.SMEM)
ANY = pl.BlockSpec(memory_space=pl.ANY)


def shards(surface, area, sea, weights, src_row, dst_tile, dst_local):
    tiles = lax.axis_size("tile")
    section = lax.axis_index("comp").astype(I32).reshape(1)
    _, fields, rows, cells = surface.shape
    blocks = weights.shape[1]
    slots = 2 * blocks // tiles
    pitch = (fields + 1) * slots
    swap = [(0, 1), (1, 0)]
    up = [(i, i + 1) for i in range(tiles - 1)]
    down = [(i + 1, i) for i in range(tiles - 1)]

    before = lax.ppermute(surface[0, :, rows - 1], "tile", up)
    after = lax.ppermute(surface[0, :, 0], "tile", down)
    area_far = lax.ppermute(area, "comp", swap)
    tile_of = dst_tile.reshape(blocks)

    sizes = dict(blocks=blocks, rows=rows, slots=slots)
    prod, part, edge_w, edges = pl.pallas_call(
        functools.partial(products_kernel, blocks=blocks, fields=fields, rows=rows),
        out_shape=(
            jax.ShapeDtypeStruct((blocks * fields, LANES), F32),
            jax.ShapeDtypeStruct((fields, LANES), F32),
            jax.ShapeDtypeStruct((EDGES, cells, cells), F32),
            jax.ShapeDtypeStruct((blocks + 8,), I32),
        ),
        in_specs=[SMEM, VMEM, VMEM, ANY],
        out_specs=(VMEM, VMEM, VMEM, SMEM),
        scratch_shapes=[
            pltpu.VMEM((blocks, cells, cells), F32),
            pltpu.VMEM((rows * fields, cells), F32),
            pltpu.VMEM((rows, 2 * SUB, cells), BF16),
            pltpu.SemaphoreType.DMA((CHUNKS,)),
        ],
        compiler_params=pltpu.CompilerParams(vmem_limit_bytes=52 << 20),
        cost_estimate=pl.CostEstimate(flops=2 * 10**8, bytes_accessed=20 << 20, transcendentals=0),
        name="products",
    )(src_row, surface, area, weights)

    packed, total = pl.pallas_call(
        functools.partial(
            pack_kernel, blocks=blocks, fields=fields, rows=rows, slots=slots, tiles=tiles
        ),
        out_shape=(
            jax.ShapeDtypeStruct((tiles * pitch, LANES), F32),
            jax.ShapeDtypeStruct((fields, LANES), F32),
        ),
        in_specs=[SMEM] * 4 + [VMEM] * 6 + [ANY],
        out_specs=(VMEM, VMEM),
        scratch_shapes=[
            pltpu.VMEM((cells, cells), F32),
            pltpu.SMEM((tiles,), I32),
            pltpu.SMEM((blocks,), I32),
            pltpu.SemaphoreType.DMA,
        ],
        compiler_params=pltpu.CompilerParams(vmem_limit_bytes=52 << 20),
        name="pack",
    )(src_row, tile_of, dst_local, edges, prod, part, edge_w, before, after, area, weights)

    recv = lax.all_to_all(packed.reshape(tiles, pitch, LANES), "tile", 0, 0, tiled=True)

    masked, tail = pl.pallas_call(
        functools.partial(place_kernel, fields=fields, rows=rows, slots=slots, tiles=tiles),
        out_shape=(
            jax.ShapeDtypeStruct((fields, rows, cells), F32),
            jax.ShapeDtypeStruct((tiles, LANES), F32),
        ),
        in_specs=[SMEM, VMEM, VMEM, VMEM, VMEM],
        out_specs=(VMEM, VMEM),
        compiler_params=pltpu.CompilerParams(vmem_limit_bytes=24 << 20),
        name="place",
    )(section, recv, total, area_far, sea)

    tail = lax.all_to_all(tail, "tile", 0, 0, tiled=True)

    out = pl.pallas_call(
        functools.partial(correct_kernel, fields=fields),
        out_shape=jax.ShapeDtypeStruct((1, fields, rows, cells), F32),
        in_specs=[SMEM, VMEM, VMEM, VMEM],
        out_specs=VMEM,
        compiler_params=pltpu.CompilerParams(vmem_limit_bytes=16 << 20),
        name="correct",
    )(section, masked, tail, sea)
    return lax.ppermute(out, "comp", swap)


def solution(mesh):
    placed = (
        P("comp", None, "tile", None),
        P("comp", "tile", None),
        P("tile", None),
        P("comp", "tile", None, None),
        P("comp", "tile"),
        P("comp", "tile", None),
        P("comp", "tile"),
    )
    return jax.shard_map(
        shards, mesh=mesh, in_specs=placed, out_specs=P("comp", None, "tile", None), check_vma=False
    )
```

```python
import functools

import jax
import jax.numpy as jnp
from jax import lax
from jax.experimental import pallas as pl
from jax.experimental.pallas import tpu as pltpu
from jax.sharding import PartitionSpec as P

RATE = 0.2
LANES = 128
SUB = 8
CHUNKS = 8
PIECES = 4

F32 = jnp.float32
BF16 = jnp.bfloat16
I32 = jnp.int32


def split_rows(rows):
    lead = rows.astype(BF16).astype(F32)
    return jnp.concatenate([lead, rows - lead], axis=0).astype(BF16)


def block_product(rows2, w):
    lead = w.astype(BF16)
    rest = (w - lead.astype(F32)).astype(BF16)
    both = jnp.concatenate([lead, rest], axis=0)
    t = lax.dot_general(rows2, both, (((1,), (1,)), ((), ())), preferred_element_type=F32)
    t = t[:, :LANES] + t[:, LANES:]
    return t[:SUB] + t[SUB:]


def prepare_kernel(
    surf_ref, area_ref, smooth_ref, part_ref, rim_ref, *, fields, rows
):
    r_iota = lax.broadcasted_iota(I32, (rows, LANES), 0)
    c_iota = lax.broadcasted_iota(I32, (rows, LANES), 1)
    area = area_ref[0]
    rim_ref[0:1, :] = area[0:1]
    rim_ref[1:2, :] = area[rows - 1 : rows]
    for f in range(fields):
        s = surf_ref[0, f]
        n = jnp.where(r_iota > 0, pltpu.roll(s, 1, 0), 0.0)
        n += jnp.where(r_iota < rows - 1, pltpu.roll(s, rows - 1, 0), 0.0)
        n += jnp.where(c_iota > 0, pltpu.roll(s, 1, 1), 0.0)
        n += jnp.where(c_iota < LANES - 1, pltpu.roll(s, LANES - 1, 1), 0.0)
        sm = s + RATE * (n - 4.0 * s)
        part_ref[pl.ds(f, 1), :] = jnp.sum(area * sm, axis=0, keepdims=True)
        smooth_ref[pl.ds(f, rows, stride=fields), :] = sm


def products_kernel(
    section_ref, code_ref, smooth_ref, part_ref, rim_ref, before_ref, after_ref, far_ref, w_hbm,
    packed_ref, total_ref, area_ref,
    spot_ref, count, wbuf, rows2, w_sems,
    *, blocks, fields, rows, slots, tiles,
):
    per = blocks // CHUNKS
    pitch = (fields + 1) * slots

    def fetch(p):
        span = pl.ds(p * (per // PIECES), per // PIECES)
        return pltpu.make_async_copy(w_hbm.at[0, span], wbuf.at[span], w_sems.at[p])

    for p in range(CHUNKS * PIECES):
        fetch(p).start()

    area_ref[...] = far_ref[...]
    before = RATE * before_ref[...]
    after = RATE * after_ref[...]
    total_ref[...] = part_ref[...] + rim_ref[0:1] * before + rim_ref[1:2] * after

    def clear(t, carry):
        count[t] = 0
        base = pl.multiple_of(t * pitch + fields * slots, SUB)
        packed_ref[pl.ds(base, slots), :] = jnp.full((slots, LANES), -1.0, F32)
        return carry

    lax.fori_loop(0, tiles, clear, 0, unroll=8)

    def number(i, carry):
        codes = [code_ref[0, i * SUB + j] for j in range(SUB)]
        for j, code in enumerate(codes):
            t = code >> 14
            rank = count[t]
            count[t] = rank + 1
            at = t * pitch + rank
            spot_ref[i * SUB + j] = at * rows + (code & (rows - 1))
            local = jnp.full((1, LANES), (code >> 7) & (rows - 1), I32)
            packed_ref[pl.ds(at + fields * slots, 1), :] = local.astype(F32)
        return carry

    lax.fori_loop(0, blocks // SUB, number, 0)

    def halves(g, carry):
        rows2[g] = split_rows(smooth_ref[pl.ds(pl.multiple_of(g * SUB, SUB), SUB), :])
        return carry

    lax.fori_loop(0, rows, halves, 0, unroll=8)
    rows2[0] = split_rows(smooth_ref[0:SUB, :] + before)
    rows2[rows - 1] = split_rows(smooth_ref[pl.ds((rows - 1) * SUB, SUB), :] + after)

    def chunk(c, carry):
        spots = [spot_ref[c * per + b] for b in range(per)]
        for p in range(PIECES):
            fetch(c * PIECES + p).wait()
        for b, spot in enumerate(spots):
            out = block_product(rows2[spot & (rows - 1)], wbuf[c * per + b])
            packed_ref[pl.ds(spot >> 7, SUB, stride=slots), :] = out
        return carry

    lax.fori_loop(0, CHUNKS, chunk, 0)


def place_kernel(
    section_ref, recv_ref, total_ref, area_ref, sea_ref, masked_ref, tail_ref,
    *, fields, rows, slots, tiles,
):
    count = tiles * slots
    target = recv_ref[:, fields * slots :, :].reshape(count, LANES)
    lane = lax.broadcasted_iota(I32, (count, rows), 1).astype(F32)
    placing = jnp.where(target == lane, 1.0, 0.0).T.astype(BF16)
    used = target >= 0.0
    mask = jnp.where(section_ref[0] == 1, 1.0, sea_ref[...].astype(F32))
    weight = area_ref[0] * mask
    lane1 = lax.broadcasted_iota(I32, (1, LANES), 1)
    tail = jnp.where(lane1 == fields, jnp.sum(weight), 0.0)
    for f in range(fields):
        x = recv_ref[:, f * slots : (f + 1) * slots, :].reshape(count, LANES)
        x = jnp.where(used, x, 0.0)
        lead = x.astype(BF16)
        rest = (x - lead.astype(F32)).astype(BF16)
        got = jnp.dot(placing, lead, preferred_element_type=F32)
        got += jnp.dot(placing, rest, preferred_element_type=F32)
        masked_ref[f] = got * mask
        gap = jnp.sum(total_ref[pl.ds(f, 1), :]) - jnp.sum(weight * got)
        tail += jnp.where(lane1 == f, gap, 0.0)
    tail_ref[...] = jnp.broadcast_to(tail, (tiles, LANES))


def correct_kernel(section_ref, masked_ref, sums_ref, sea_ref, out_ref, *, fields):
    sums = sums_ref[...]
    lane1 = lax.broadcasted_iota(I32, (1, LANES), 1)
    whole = jnp.sum(jnp.where(lane1 == fields, sums, 0.0), axis=1, keepdims=True)
    deficit = sums / whole
    mask = jnp.where(section_ref[0] == 0, 1.0, sea_ref[...].astype(F32))
    for f in range(fields):
        d = jnp.sum(jnp.where(lane1 == f, deficit, 0.0), axis=1, keepdims=True)
        out_ref[0, f] = masked_ref[f] + mask * d


VMEM = pl.BlockSpec(memory_space=pltpu.VMEM)
SMEM = pl.BlockSpec(memory_space=pltpu.SMEM)
HBM = pl.BlockSpec(memory_space=pltpu.HBM)


def shards(surface, area, sea, weights, src_row, dst_tile, dst_local):
    tiles = lax.axis_size("tile")
    section = lax.axis_index("comp").astype(I32).reshape(1)
    _, fields, rows, cells = surface.shape
    blocks = weights.shape[1]
    slots = 2 * blocks // tiles
    pitch = (fields + 1) * slots
    swap = [(0, 1), (1, 0)]
    up = [(i, i + 1) for i in range(tiles - 1)]
    down = [(i + 1, i) for i in range(tiles - 1)]

    before = lax.ppermute(surface[0, :, rows - 1], "tile", up)
    after = lax.ppermute(surface[0, :, 0], "tile", down)
    area_far = lax.ppermute(area, "comp", swap)
    code = (dst_tile[:, :, 0] << 14) | (dst_local << 7) | src_row

    sizes = dict(blocks=blocks, fields=fields, rows=rows, slots=slots, tiles=tiles)
    smooth, part, rim = pl.pallas_call(
        functools.partial(prepare_kernel, fields=fields, rows=rows),
        out_shape=(
            jax.ShapeDtypeStruct((rows * fields, LANES), F32),
            jax.ShapeDtypeStruct((fields, LANES), F32),
            jax.ShapeDtypeStruct((SUB, LANES), F32),
        ),
        in_specs=[VMEM, VMEM],
        out_specs=(VMEM, VMEM, VMEM),
        compiler_params=pltpu.CompilerParams(vmem_limit_bytes=8 << 20),
        cost_estimate=pl.CostEstimate(flops=10**7, bytes_accessed=8 << 20, transcendentals=0),
        name="prepare",
    )(surface, area)

    packed, total, area_far = pl.pallas_call(
        functools.partial(products_kernel, **sizes),
        out_shape=(
            jax.ShapeDtypeStruct((tiles * pitch, LANES), F32),
            jax.ShapeDtypeStruct((fields, LANES), F32),
            jax.ShapeDtypeStruct((1, rows, cells), F32),
        ),
        in_specs=[SMEM] * 2 + [VMEM] * 6 + [HBM],
        out_specs=(VMEM, VMEM, VMEM),
        scratch_shapes=[
            pltpu.SMEM((blocks,), I32),
            pltpu.SMEM((tiles,), I32),
            pltpu.VMEM((blocks, cells, cells), F32),
            pltpu.VMEM((rows, 2 * SUB, cells), BF16),
            pltpu.SemaphoreType.DMA((CHUNKS * PIECES,)),
        ],
        compiler_params=pltpu.CompilerParams(vmem_limit_bytes=46 << 20),
        cost_estimate=pl.CostEstimate(flops=2 * 10**8, bytes_accessed=20 << 20, transcendentals=0),
        name="products",
    )(section, code, smooth, part, rim, before, after, area_far, weights)

    recv = lax.all_to_all(packed.reshape(tiles, pitch, LANES), "tile", 0, 0, tiled=True)

    masked, tail = pl.pallas_call(
        functools.partial(place_kernel, fields=fields, rows=rows, slots=slots, tiles=tiles),
        out_shape=(
            jax.ShapeDtypeStruct((fields, rows, cells), F32),
            jax.ShapeDtypeStruct((tiles, LANES), F32),
        ),
        in_specs=[SMEM, VMEM, VMEM, VMEM, VMEM],
        out_specs=(VMEM, VMEM),
        compiler_params=pltpu.CompilerParams(vmem_limit_bytes=24 << 20),
        name="place",
    )(section, recv, total, area_far, sea)

    masked = lax.ppermute(masked, "comp", swap)
    tail = lax.all_to_all(tail, "tile", 0, 0, tiled=True)
    sums = lax.ppermute(jnp.sum(tail, axis=0, keepdims=True), "comp", swap)

    return pl.pallas_call(
        functools.partial(correct_kernel, fields=fields),
        out_shape=jax.ShapeDtypeStruct((1, fields, rows, cells), F32),
        in_specs=[SMEM, VMEM, VMEM, VMEM],
        out_specs=VMEM,
        compiler_params=pltpu.CompilerParams(vmem_limit_bytes=16 << 20),
        name="correct",
    )(section, masked, sums, sea)


def solution(mesh):
    placed = (
        P("comp", None, "tile", None),
        P("comp", "tile", None),
        P("tile", None),
        P("comp", "tile", None, None),
        P("comp", "tile"),
        P("comp", "tile", None),
        P("comp", "tile"),
    )
    return jax.shard_map(
        shards, mesh=mesh, in_specs=placed, out_specs=P("comp", None, "tile", None), check_vma=False
    )
```

```python
import functools

import jax
import jax.numpy as jnp
from jax import lax
from jax.experimental import pallas as pl
from jax.experimental.pallas import tpu as pltpu
from jax.sharding import PartitionSpec as P

RATE = 0.2
LANES = 128
SUB = 8
CHUNKS = 8
PIECES = 2

F32 = jnp.float32
BF16 = jnp.bfloat16
I32 = jnp.int32


def split_rows(rows):
    lead = rows.astype(BF16).astype(F32)
    return jnp.concatenate([lead, rows - lead], axis=0).astype(BF16)


def block_product(rows2, w):
    lead = w.astype(BF16)
    rest = (w - lead.astype(F32)).astype(BF16)
    both = jnp.concatenate([lead, rest], axis=0)
    t = lax.dot_general(rows2, both, (((1,), (1,)), ((), ())), preferred_element_type=F32)
    t = t[:, :LANES] + t[:, LANES:]
    return t[:SUB] + t[SUB:]


def prepare_kernel(
    surf_ref, area_ref, smooth_ref, part_ref, rim_ref, *, fields, rows
):
    r_iota = lax.broadcasted_iota(I32, (rows, LANES), 0)
    c_iota = lax.broadcasted_iota(I32, (rows, LANES), 1)
    area = area_ref[0]
    rim_ref[0:1, :] = area[0:1]
    rim_ref[1:2, :] = area[rows - 1 : rows]
    for f in range(fields):
        s = surf_ref[0, f]
        n = jnp.where(r_iota > 0, pltpu.roll(s, 1, 0), 0.0)
        n += jnp.where(r_iota < rows - 1, pltpu.roll(s, rows - 1, 0), 0.0)
        n += jnp.where(c_iota > 0, pltpu.roll(s, 1, 1), 0.0)
        n += jnp.where(c_iota < LANES - 1, pltpu.roll(s, LANES - 1, 1), 0.0)
        sm = s + RATE * (n - 4.0 * s)
        part_ref[pl.ds(f, 1), :] = jnp.sum(area * sm, axis=0, keepdims=True)
        smooth_ref[pl.ds(f, rows, stride=fields), :] = sm


def products_kernel(
    section_ref, code_ref, smooth_ref, part_ref, rim_ref, before_ref, after_ref, far_ref, w_hbm,
    packed_ref, total_ref, area_ref,
    spot_ref, count, index, wbuf, rows2, w_sems,
    *, blocks, fields, rows, slots, tiles,
):
    per = blocks // CHUNKS
    pitch = fields * slots + 1

    def fetch(p):
        span = pl.ds(p * (per // PIECES), per // PIECES)
        return pltpu.make_async_copy(w_hbm.at[0, span], wbuf.at[span], w_sems.at[p])

    for p in range(CHUNKS * PIECES):
        fetch(p).start()

    area_ref[...] = far_ref[...]
    before = RATE * before_ref[...]
    after = RATE * after_ref[...]
    total_ref[...] = part_ref[...] + rim_ref[0:1] * before + rim_ref[1:2] * after

    def clear(t, carry):
        count[t] = 0
        return carry

    lax.fori_loop(0, tiles, clear, 0, unroll=8)
    index[...] = jnp.full((tiles * slots, LANES), -1.0, F32)

    def number(i, carry):
        codes = [code_ref[0, i * SUB + j] for j in range(SUB)]
        for j, code in enumerate(codes):
            t = code >> 14
            rank = count[t]
            count[t] = rank + 1
            spot_ref[i * SUB + j] = (t * pitch + rank) * rows + (code & (rows - 1))
            local = jnp.full((1, LANES), (code >> 7) & (rows - 1), I32)
            index[pl.ds(t * slots + rank, 1), :] = local.astype(F32)
        return carry

    lax.fori_loop(0, blocks // SUB, number, 0)
    slot = lax.broadcasted_iota(I32, (tiles, slots, LANES), 1)
    lane = lax.broadcasted_iota(I32, (tiles, slots, LANES), 2)
    own = jnp.where(slot == lane, index[...].reshape(tiles, slots, LANES), 0.0)
    packed_ref[pl.ds(fields * slots, tiles, stride=pitch), :] = jnp.sum(own, axis=1)

    def halves(g, carry):
        rows2[g] = split_rows(smooth_ref[pl.ds(pl.multiple_of(g * SUB, SUB), SUB), :])
        return carry

    lax.fori_loop(0, rows, halves, 0, unroll=8)
    rows2[0] = split_rows(smooth_ref[0:SUB, :] + before)
    rows2[rows - 1] = split_rows(smooth_ref[pl.ds((rows - 1) * SUB, SUB), :] + after)

    def chunk(c, carry):
        spots = [spot_ref[c * per + b] for b in range(per)]
        for p in range(PIECES):
            fetch(c * PIECES + p).wait()
        for b, spot in enumerate(spots):
            out = block_product(rows2[spot & (rows - 1)], wbuf[c * per + b])
            packed_ref[pl.ds(spot >> 7, SUB, stride=slots), :] = out
        return carry

    lax.fori_loop(0, CHUNKS, chunk, 0)


def place_kernel(
    section_ref, recv_ref, total_ref, area_ref, sea_ref, masked_ref, tail_ref,
    *, fields, rows, slots, tiles,
):
    pitch = fields * slots + 1
    targets = recv_ref[pl.ds(fields * slots, tiles, stride=pitch), :]
    lane = lax.broadcasted_iota(I32, (tiles, rows), 1).astype(F32)
    target = jnp.concatenate(
        [jnp.broadcast_to(targets[:, j : j + 1], (tiles, rows)) for j in range(slots)], axis=0
    )
    placing = jnp.where(target == jnp.concatenate([lane] * slots, axis=0), 1.0, 0.0).T.astype(BF16)
    used = target >= 0.0
    mask = jnp.where(section_ref[0] == 1, 1.0, sea_ref[...].astype(F32))
    weight = area_ref[0] * mask
    lane1 = lax.broadcasted_iota(I32, (1, LANES), 1)
    tail = jnp.where(lane1 == fields, jnp.sum(weight), 0.0)
    for f in range(fields):
        x = jnp.concatenate(
            [recv_ref[pl.ds(f * slots + j, tiles, stride=pitch), :] for j in range(slots)], axis=0
        )
        x = jnp.where(used, x, 0.0)
        lead = x.astype(BF16)
        rest = (x - lead.astype(F32)).astype(BF16)
        got = jnp.dot(placing, lead, preferred_element_type=F32)
        got += jnp.dot(placing, rest, preferred_element_type=F32)
        masked_ref[f] = got * mask
        gap = jnp.sum(total_ref[pl.ds(f, 1), :]) - jnp.sum(weight * got)
        tail += jnp.where(lane1 == f, gap, 0.0)
    tail_ref[...] = jnp.broadcast_to(tail, (tiles, LANES))


def correct_kernel(section_ref, masked_ref, sums_ref, sea_ref, out_ref, *, fields):
    sums = sums_ref[...]
    lane1 = lax.broadcasted_iota(I32, (1, LANES), 1)
    whole = jnp.sum(jnp.where(lane1 == fields, sums, 0.0), axis=1, keepdims=True)
    deficit = sums / whole
    mask = jnp.where(section_ref[0] == 0, 1.0, sea_ref[...].astype(F32))
    for f in range(fields):
        d = jnp.sum(jnp.where(lane1 == f, deficit, 0.0), axis=1, keepdims=True)
        out_ref[0, f] = masked_ref[f] + mask * d


VMEM = pl.BlockSpec(memory_space=pltpu.VMEM)
SMEM = pl.BlockSpec(memory_space=pltpu.SMEM)
HBM = pl.BlockSpec(memory_space=pltpu.HBM)


def shards(surface, area, sea, weights, src_row, dst_tile, dst_local):
    tiles = lax.axis_size("tile")
    section = lax.axis_index("comp").astype(I32).reshape(1)
    _, fields, rows, cells = surface.shape
    blocks = weights.shape[1]
    slots = 2 * blocks // tiles
    pitch = fields * slots + 1
    swap = [(0, 1), (1, 0)]
    up = [(i, i + 1) for i in range(tiles - 1)]
    down = [(i + 1, i) for i in range(tiles - 1)]

    before = lax.ppermute(surface[0, :, rows - 1], "tile", up)
    after = lax.ppermute(surface[0, :, 0], "tile", down)
    area_far = lax.ppermute(area, "comp", swap)
    code = (dst_tile[:, :, 0] << 14) | (dst_local << 7) | src_row

    sizes = dict(blocks=blocks, fields=fields, rows=rows, slots=slots, tiles=tiles)
    smooth, part, rim = pl.pallas_call(
        functools.partial(prepare_kernel, fields=fields, rows=rows),
        out_shape=(
            jax.ShapeDtypeStruct((rows * fields, LANES), F32),
            jax.ShapeDtypeStruct((fields, LANES), F32),
            jax.ShapeDtypeStruct((SUB, LANES), F32),
        ),
        in_specs=[VMEM, VMEM],
        out_specs=(VMEM, VMEM, VMEM),
        compiler_params=pltpu.CompilerParams(vmem_limit_bytes=8 << 20),
        cost_estimate=pl.CostEstimate(flops=10**7, bytes_accessed=8 << 20, transcendentals=0),
        name="prepare",
    )(surface, area)

    packed, total, area_far = pl.pallas_call(
        functools.partial(products_kernel, **sizes),
        out_shape=(
            jax.ShapeDtypeStruct((tiles * pitch, LANES), F32),
            jax.ShapeDtypeStruct((fields, LANES), F32),
            jax.ShapeDtypeStruct((1, rows, cells), F32),
        ),
        in_specs=[SMEM] * 2 + [VMEM] * 6 + [HBM],
        out_specs=(VMEM, VMEM, VMEM),
        scratch_shapes=[
            pltpu.SMEM((blocks,), I32),
            pltpu.SMEM((tiles,), I32),
            pltpu.VMEM((tiles * slots, LANES), F32),
            pltpu.VMEM((blocks, cells, cells), F32),
            pltpu.VMEM((rows, 2 * SUB, cells), BF16),
            pltpu.SemaphoreType.DMA((CHUNKS * PIECES,)),
        ],
        compiler_params=pltpu.CompilerParams(vmem_limit_bytes=46 << 20),
        cost_estimate=pl.CostEstimate(flops=2 * 10**8, bytes_accessed=20 << 20, transcendentals=0),
        name="products",
    )(section, code, smooth, part, rim, before, after, area_far, weights)

    flat = packed.reshape(tiles, 1, pitch * LANES)
    recv = lax.all_to_all(flat, "tile", 0, 0, tiled=True).reshape(tiles * pitch, LANES)

    masked, tail = pl.pallas_call(
        functools.partial(place_kernel, fields=fields, rows=rows, slots=slots, tiles=tiles),
        out_shape=(
            jax.ShapeDtypeStruct((fields, rows, cells), F32),
            jax.ShapeDtypeStruct((tiles, LANES), F32),
        ),
        in_specs=[SMEM, VMEM, VMEM, VMEM, VMEM],
        out_specs=(VMEM, VMEM),
        compiler_params=pltpu.CompilerParams(vmem_limit_bytes=24 << 20),
        name="place",
    )(section, recv, total, area_far, sea)

    masked = lax.ppermute(masked, "comp", swap)
    tail = lax.all_to_all(tail, "tile", 0, 0, tiled=True)
    sums = lax.ppermute(jnp.sum(tail, axis=0, keepdims=True), "comp", swap)

    return pl.pallas_call(
        functools.partial(correct_kernel, fields=fields),
        out_shape=jax.ShapeDtypeStruct((1, fields, rows, cells), F32),
        in_specs=[SMEM, VMEM, VMEM, VMEM],
        out_specs=VMEM,
        compiler_params=pltpu.CompilerParams(vmem_limit_bytes=16 << 20),
        name="correct",
    )(section, masked, sums, sea)


def solution(mesh):
    placed = (
        P("comp", None, "tile", None),
        P("comp", "tile", None),
        P("tile", None),
        P("comp", "tile", None, None),
        P("comp", "tile"),
        P("comp", "tile", None),
        P("comp", "tile"),
    )
    return jax.shard_map(
        shards, mesh=mesh, in_specs=placed, out_specs=P("comp", None, "tile", None), check_vma=False
    )
```

```python
import functools

import jax
import jax.numpy as jnp
from jax import lax
from jax.experimental import pallas as pl
from jax.experimental.pallas import tpu as pltpu
from jax.sharding import PartitionSpec as P

RATE = 0.2
LANES = 128
SUB = 8
CHUNKS = 8
PIECES = 2
EARLY = 4

F32 = jnp.float32
BF16 = jnp.bfloat16
I32 = jnp.int32


def split_rows(rows):
    lead = rows.astype(BF16).astype(F32)
    return jnp.concatenate([lead, rows - lead], axis=0).astype(BF16)


def block_product(rows2, w):
    lead = w.astype(BF16)
    rest = (w - lead.astype(F32)).astype(BF16)
    both = jnp.concatenate([lead, rest], axis=0)
    t = lax.dot_general(rows2, both, (((1,), (1,)), ((), ())), preferred_element_type=F32)
    t = t[:, :LANES] + t[:, LANES:]
    return t[:SUB] + t[SUB:]


def prepare_kernel(
    code_ref, surf_ref, w_hbm,
    smooth_ref, w_ref, spot_ref, targets_ref,
    sems, *, blocks, fields, rows, slots, tiles,
):
    size = w_ref.shape[0] // EARLY
    copies = [
        pltpu.make_async_copy(
            w_hbm.at[0, pl.ds(p * size, size)], w_ref.at[pl.ds(p * size, size)], sems.at[p]
        )
        for p in range(EARLY)
    ]
    for copy in copies:
        copy.start()
    r_iota = lax.broadcasted_iota(I32, (rows, LANES), 0)
    c_iota = lax.broadcasted_iota(I32, (rows, LANES), 1)
    for f in range(fields):
        s = surf_ref[0, f]
        n = jnp.where(r_iota > 0, pltpu.roll(s, 1, 0), 0.0)
        n += jnp.where(r_iota < rows - 1, pltpu.roll(s, rows - 1, 0), 0.0)
        n += jnp.where(c_iota > 0, pltpu.roll(s, 1, 1), 0.0)
        n += jnp.where(c_iota < LANES - 1, pltpu.roll(s, LANES - 1, 1), 0.0)
        sm = s + RATE * (n - 4.0 * s)
        smooth_ref[pl.ds(f, rows, stride=fields), :] = sm

    pitch = fields * slots + 1
    code = code_ref[...]
    tile = (code >> 14).astype(F32)
    local = ((code >> 7) & (rows - 1)).astype(F32)

    def column(v):
        parts = [v[:, i : i + LANES] for i in range(0, blocks, LANES)]
        return jnp.concatenate([jnp.broadcast_to(p, (LANES, LANES)).T for p in parts], axis=0)

    def ones(mask):
        return jnp.where(mask, 1.0, 0.0).astype(BF16)

    def count(a, b):
        return jnp.dot(a, b, preferred_element_type=F32)

    down = lax.broadcasted_iota(I32, (blocks, blocks), 0)
    right = lax.broadcasted_iota(I32, (blocks, blocks), 1)
    same = jnp.concatenate([column(tile)] * (blocks // LANES), axis=1) == tile
    rank = count(jnp.ones((SUB, blocks), BF16), ones(same & (down < right)))[0:1]
    rank_down = count(ones(same & (right < down)), jnp.ones((blocks, LANES), BF16))
    spot_ref[...] = ((code >> 14) * pitch + rank.astype(I32)) * rows + (code & (rows - 1))
    tiles_down = lax.broadcasted_iota(I32, (tiles, blocks), 0).astype(F32)
    lane = lax.broadcasted_iota(I32, (blocks, LANES), 1).astype(F32)
    value = jnp.where(lane == rank_down, column(local) + 1.0, 0.0).astype(BF16)
    targets_ref[...] = count(ones(tiles_down == tile), value) - 1.0

    for copy in copies:
        copy.wait()


def products_kernel(
    section_ref, spot_ref, targets_ref, smooth_ref, before_ref, after_ref, far_ref, early_ref,
    w_hbm,
    packed_ref, area_ref, rim_ref,
    wbuf, rows2, w_sems,
    *, blocks, fields, rows, slots, tiles,
):
    per = blocks // CHUNKS
    pitch = fields * slots + 1

    size = per // PIECES

    def fetch(p):
        return pltpu.make_async_copy(
            w_hbm.at[0, pl.ds(per + p * size, size)], wbuf.at[pl.ds(p * size, size)], w_sems.at[p]
        )

    for p in range((CHUNKS - 1) * PIECES):
        fetch(p).start()

    area_ref[...] = far_ref[...]
    before = RATE * before_ref[...]
    after = RATE * after_ref[...]
    rim_ref[0] = before
    rim_ref[1] = after

    packed_ref[pl.ds(fields * slots, tiles, stride=pitch), :] = targets_ref[...]

    def halves(g, carry):
        rows2[g] = split_rows(smooth_ref[pl.ds(pl.multiple_of(g * SUB, SUB), SUB), :])
        return carry

    lax.fori_loop(0, rows, halves, 0, unroll=8)
    rows2[0] = split_rows(smooth_ref[0:SUB, :] + before)
    rows2[rows - 1] = split_rows(smooth_ref[pl.ds((rows - 1) * SUB, SUB), :] + after)

    def chunk(c, w_ref):
        spots = [spot_ref[0, c * per + b] for b in range(per)]
        for b, spot in enumerate(spots):
            out = block_product(rows2[spot & (rows - 1)], w_ref[b])
            packed_ref[pl.ds(spot >> 7, SUB, stride=slots), :] = out

    def later(c, carry):
        for p in range(PIECES):
            fetch(c * PIECES + p).wait()
        chunk(c + 1, wbuf.at[pl.ds(c * per, per)])
        return carry

    chunk(0, early_ref)
    lax.fori_loop(0, CHUNKS - 1, later, 0)


def place_kernel(
    section_ref, recv_ref, smooth_ref, rim_ref, own_ref, area_ref, sea_ref, masked_ref, tail_ref,
    *, fields, rows, slots, tiles,
):
    pitch = fields * slots + 1
    targets = recv_ref[pl.ds(fields * slots, tiles, stride=pitch), :]
    lane = lax.broadcasted_iota(I32, (tiles, rows), 1).astype(F32)
    target = jnp.concatenate(
        [jnp.broadcast_to(targets[:, j : j + 1], (tiles, rows)) for j in range(slots)], axis=0
    )
    placing = jnp.where(target == jnp.concatenate([lane] * slots, axis=0), 1.0, 0.0).T.astype(BF16)
    used = target >= 0.0
    mask = jnp.where(section_ref[0] == 1, 1.0, sea_ref[...].astype(F32))
    weight = area_ref[0] * mask
    own = own_ref[0]
    lane1 = lax.broadcasted_iota(I32, (1, LANES), 1)
    tail = jnp.where(lane1 == fields, jnp.sum(weight), 0.0)
    for f in range(fields):
        x = jnp.concatenate(
            [recv_ref[pl.ds(f * slots + j, tiles, stride=pitch), :] for j in range(slots)], axis=0
        )
        x = jnp.where(used, x, 0.0)
        lead = x.astype(BF16)
        rest = (x - lead.astype(F32)).astype(BF16)
        got = jnp.dot(placing, lead, preferred_element_type=F32)
        got += jnp.dot(placing, rest, preferred_element_type=F32)
        masked_ref[f] = got * mask
        source = own * smooth_ref[pl.ds(f, rows, stride=fields), :]
        edge = own[0:1] * rim_ref[0, f : f + 1] + own[rows - 1 : rows] * rim_ref[1, f : f + 1]
        gap = jnp.sum(source - weight * got) + jnp.sum(edge)
        tail += jnp.where(lane1 == f, gap, 0.0)
    tail_ref[...] = jnp.broadcast_to(tail, (tiles, LANES))


def correct_kernel(section_ref, masked_ref, sums_ref, sea_ref, out_ref, *, fields):
    sums = sums_ref[...]
    lane1 = lax.broadcasted_iota(I32, (1, LANES), 1)
    whole = jnp.sum(jnp.where(lane1 == fields, sums, 0.0), axis=1, keepdims=True)
    deficit = sums / whole
    mask = jnp.where(section_ref[0] == 0, 1.0, sea_ref[...].astype(F32))
    for f in range(fields):
        d = jnp.sum(jnp.where(lane1 == f, deficit, 0.0), axis=1, keepdims=True)
        out_ref[0, f] = masked_ref[f] + mask * d


VMEM = pl.BlockSpec(memory_space=pltpu.VMEM)
SMEM = pl.BlockSpec(memory_space=pltpu.SMEM)
HBM = pl.BlockSpec(memory_space=pltpu.HBM)


def shards(surface, area, sea, weights, src_row, dst_tile, dst_local):
    tiles = lax.axis_size("tile")
    section = lax.axis_index("comp").astype(I32).reshape(1)
    _, fields, rows, cells = surface.shape
    blocks = weights.shape[1]
    slots = 2 * blocks // tiles
    pitch = fields * slots + 1
    swap = [(0, 1), (1, 0)]
    up = [(i, i + 1) for i in range(tiles - 1)]
    down = [(i + 1, i) for i in range(tiles - 1)]

    before = lax.ppermute(surface[0, :, rows - 1], "tile", up)
    after = lax.ppermute(surface[0, :, 0], "tile", down)
    area_far = lax.ppermute(area, "comp", swap)
    code = (dst_tile[:, :, 0] << 14) | (dst_local << 7) | src_row

    sizes = dict(blocks=blocks, fields=fields, rows=rows, slots=slots, tiles=tiles)
    smooth, early, spot, targets = pl.pallas_call(
        functools.partial(prepare_kernel, **sizes),
        out_shape=(
            jax.ShapeDtypeStruct((rows * fields, LANES), F32),
            jax.ShapeDtypeStruct((blocks // CHUNKS, cells, cells), F32),
            jax.ShapeDtypeStruct((1, blocks), I32),
            jax.ShapeDtypeStruct((tiles, LANES), F32),
        ),
        in_specs=[VMEM, VMEM, HBM],
        out_specs=(VMEM,) * 4,
        scratch_shapes=[pltpu.SemaphoreType.DMA((EARLY,))],
        compiler_params=pltpu.CompilerParams(vmem_limit_bytes=46 << 20),
        cost_estimate=pl.CostEstimate(flops=10**7, bytes_accessed=8 << 20, transcendentals=0),
        name="prepare",
    )(code, surface, weights)

    packed, area_far, rim = pl.pallas_call(
        functools.partial(products_kernel, **sizes),
        out_shape=(
            jax.ShapeDtypeStruct((tiles * pitch, LANES), F32),
            jax.ShapeDtypeStruct((1, rows, cells), F32),
            jax.ShapeDtypeStruct((2, fields, LANES), F32),
        ),
        in_specs=[SMEM] * 2 + [VMEM] * 6 + [HBM],
        out_specs=(VMEM, VMEM, VMEM),
        scratch_shapes=[
            pltpu.VMEM((blocks - blocks // CHUNKS, cells, cells), F32),
            pltpu.VMEM((rows, 2 * SUB, cells), BF16),
            pltpu.SemaphoreType.DMA(((CHUNKS - 1) * PIECES,)),
        ],
        compiler_params=pltpu.CompilerParams(vmem_limit_bytes=46 << 20),
        cost_estimate=pl.CostEstimate(flops=2 * 10**8, bytes_accessed=20 << 20, transcendentals=0),
        name="products",
    )(section, spot, targets, smooth, before, after, area_far, early, weights)

    flat = packed.reshape(tiles, 1, pitch * LANES)
    recv = lax.all_to_all(flat, "tile", 0, 0, tiled=True).reshape(tiles * pitch, LANES)

    masked, tail = pl.pallas_call(
        functools.partial(place_kernel, fields=fields, rows=rows, slots=slots, tiles=tiles),
        out_shape=(
            jax.ShapeDtypeStruct((fields, rows, cells), F32),
            jax.ShapeDtypeStruct((tiles, LANES), F32),
        ),
        in_specs=[SMEM] + [VMEM] * 6,
        out_specs=(VMEM, VMEM),
        compiler_params=pltpu.CompilerParams(vmem_limit_bytes=24 << 20),
        name="place",
    )(section, recv, smooth, rim, area, area_far, sea)

    masked = lax.ppermute(masked, "comp", swap)
    tail = lax.all_to_all(tail, "tile", 0, 0, tiled=True)
    sums = lax.ppermute(jnp.sum(tail, axis=0, keepdims=True), "comp", swap)

    return pl.pallas_call(
        functools.partial(correct_kernel, fields=fields),
        out_shape=jax.ShapeDtypeStruct((1, fields, rows, cells), F32),
        in_specs=[SMEM, VMEM, VMEM, VMEM],
        out_specs=VMEM,
        compiler_params=pltpu.CompilerParams(vmem_limit_bytes=16 << 20),
        name="correct",
    )(section, masked, sums, sea)


def solution(mesh):
    placed = (
        P("comp", None, "tile", None),
        P("comp", "tile", None),
        P("tile", None),
        P("comp", "tile", None, None),
        P("comp", "tile"),
        P("comp", "tile", None),
        P("comp", "tile"),
    )
    return jax.shard_map(
        shards, mesh=mesh, in_specs=placed, out_specs=P("comp", None, "tile", None), check_vma=False
    )
```

```python
import functools

import jax
import jax.numpy as jnp
from jax import lax
from jax.experimental import pallas as pl
from jax.experimental.pallas import tpu as pltpu
from jax.sharding import PartitionSpec as P

RATE = 0.2
LANES = 128
SUB = 8
CHUNKS = 8
PIECES = 2
EARLY = 4

F32 = jnp.float32
BF16 = jnp.bfloat16
I32 = jnp.int32


def split_rows(rows):
    lead = rows.astype(BF16).astype(F32)
    return jnp.concatenate([lead, rows - lead], axis=0).astype(BF16)


def block_product(rows2, w):
    lead = w.astype(BF16)
    rest = (w - lead.astype(F32)).astype(BF16)
    both = jnp.concatenate([lead, rest], axis=0)
    t = lax.dot_general(rows2, both, (((1,), (1,)), ((), ())), preferred_element_type=F32)
    t = t[:, :LANES] + t[:, LANES:]
    return t[:SUB] + t[SUB:]


def prepare_kernel(
    code_ref, surf_ref, w_hbm,
    smooth_ref, w_ref, spot_ref, targets_ref,
    sems, *, blocks, fields, rows, slots, tiles,
):
    size = w_ref.shape[0] // EARLY
    copies = [
        pltpu.make_async_copy(
            w_hbm.at[0, pl.ds(p * size, size)], w_ref.at[pl.ds(p * size, size)], sems.at[p]
        )
        for p in range(EARLY)
    ]
    for copy in copies:
        copy.start()
    r_iota = lax.broadcasted_iota(I32, (rows, LANES), 0)
    c_iota = lax.broadcasted_iota(I32, (rows, LANES), 1)
    for f in range(fields):
        s = surf_ref[0, f]
        n = jnp.where(r_iota > 0, pltpu.roll(s, 1, 0), 0.0)
        n += jnp.where(r_iota < rows - 1, pltpu.roll(s, rows - 1, 0), 0.0)
        n += jnp.where(c_iota > 0, pltpu.roll(s, 1, 1), 0.0)
        n += jnp.where(c_iota < LANES - 1, pltpu.roll(s, LANES - 1, 1), 0.0)
        sm = s + RATE * (n - 4.0 * s)
        smooth_ref[pl.ds(f, rows, stride=fields), :] = sm

    pitch = fields * slots + 1
    code = code_ref[...]
    tile = (code >> 14).astype(F32)
    local = ((code >> 7) & (rows - 1)).astype(F32)

    def column(v):
        parts = [v[:, i : i + LANES] for i in range(0, blocks, LANES)]
        return jnp.concatenate([jnp.broadcast_to(p, (LANES, LANES)).T for p in parts], axis=0)

    def ones(mask):
        return jnp.where(mask, 1.0, 0.0).astype(BF16)

    def count(a, b):
        return jnp.dot(a, b, preferred_element_type=F32)

    down = lax.broadcasted_iota(I32, (blocks, blocks), 0)
    right = lax.broadcasted_iota(I32, (blocks, blocks), 1)
    same = jnp.concatenate([column(tile)] * (blocks // LANES), axis=1) == tile
    rank = count(jnp.ones((SUB, blocks), BF16), ones(same & (down < right)))[0:1]
    rank_down = count(ones(same & (right < down)), jnp.ones((blocks, LANES), BF16))
    spot_ref[...] = ((code >> 14) * pitch + rank.astype(I32)) * rows + (code & (rows - 1))
    tiles_down = lax.broadcasted_iota(I32, (tiles, blocks), 0).astype(F32)
    lane = lax.broadcasted_iota(I32, (blocks, LANES), 1).astype(F32)
    value = jnp.where(lane == rank_down, column(local) + 1.0, 0.0).astype(BF16)
    targets_ref[...] = count(ones(tiles_down == tile), value) - 1.0

    for copy in copies:
        copy.wait()


def products_kernel(
    section_ref, spot_ref, targets_ref, smooth_ref, before_ref, after_ref, far_ref, early_ref,
    w_hbm,
    packed_ref, area_ref, rim_ref,
    wbuf, rows2, w_sems,
    *, blocks, fields, rows, slots, tiles,
):
    per = blocks // CHUNKS
    pitch = fields * slots + 1

    size = per // PIECES

    def fetch(p):
        return pltpu.make_async_copy(
            w_hbm.at[0, pl.ds(per + p * size, size)], wbuf.at[pl.ds(p * size, size)], w_sems.at[p]
        )

    for p in range((CHUNKS - 1) * PIECES):
        fetch(p).start()

    area_ref[...] = far_ref[...]
    before = RATE * before_ref[...]
    after = RATE * after_ref[...]
    rim_ref[0] = before
    rim_ref[1] = after

    packed_ref[pl.ds(fields * slots, tiles, stride=pitch), :] = targets_ref[...]

    def halves(g, carry):
        rows2[g] = split_rows(smooth_ref[pl.ds(pl.multiple_of(g * SUB, SUB), SUB), :])
        return carry

    lax.fori_loop(0, rows, halves, 0, unroll=8)
    rows2[0] = split_rows(smooth_ref[0:SUB, :] + before)
    rows2[rows - 1] = split_rows(smooth_ref[pl.ds((rows - 1) * SUB, SUB), :] + after)

    def chunk(c, w_ref):
        spots = [spot_ref[0, c * per + b] for b in range(per)]
        for b, spot in enumerate(spots):
            out = block_product(rows2[spot & (rows - 1)], w_ref[b])
            packed_ref[pl.ds(spot >> 7, SUB, stride=slots), :] = out

    def later(c, carry):
        for p in range(PIECES):
            fetch(c * PIECES + p).wait()
        chunk(c + 1, wbuf.at[pl.ds(c * per, per)])
        return carry

    chunk(0, early_ref)
    lax.fori_loop(0, CHUNKS - 1, later, 0)


def place_kernel(
    section_ref, recv_ref, smooth_ref, rim_ref, own_ref, area_ref, sea_ref, masked_ref, tail_ref,
    *, fields, rows, slots, tiles,
):
    pitch = fields * slots + 1
    targets = recv_ref[pl.ds(fields * slots, tiles, stride=pitch), :]
    lane = lax.broadcasted_iota(I32, (tiles, rows), 1).astype(F32)
    target = jnp.concatenate(
        [jnp.broadcast_to(targets[:, j : j + 1], (tiles, rows)) for j in range(slots)], axis=0
    )
    placing = jnp.where(target == jnp.concatenate([lane] * slots, axis=0), 1.0, 0.0).T.astype(BF16)
    used = target >= 0.0
    mask = jnp.where(section_ref[0] == 1, 1.0, sea_ref[...].astype(F32))
    weight = area_ref[0] * mask
    own = own_ref[0]
    lane1 = lax.broadcasted_iota(I32, (1, LANES), 1)
    tail = jnp.where(lane1 == fields, jnp.sum(weight), 0.0)
    for f in range(fields):
        x = jnp.concatenate(
            [recv_ref[pl.ds(f * slots + j, tiles, stride=pitch), :] for j in range(slots)], axis=0
        )
        x = jnp.where(used, x, 0.0)
        lead = x.astype(BF16)
        rest = (x - lead.astype(F32)).astype(BF16)
        got = jnp.dot(placing, lead, preferred_element_type=F32)
        got += jnp.dot(placing, rest, preferred_element_type=F32)
        masked_ref[f] = got * mask
        source = own * smooth_ref[pl.ds(f, rows, stride=fields), :]
        edge = own[0:1] * rim_ref[0, f : f + 1] + own[rows - 1 : rows] * rim_ref[1, f : f + 1]
        gap = jnp.sum(source - weight * got) + jnp.sum(edge)
        tail += jnp.where(lane1 == f, gap, 0.0)
    tail_ref[...] = jnp.broadcast_to(tail, (2 * tiles, LANES))


def correct_kernel(section_ref, masked_ref, sums_ref, sea_ref, out_ref, *, fields):
    half = sums_ref.shape[0] // 2
    near = jnp.sum(sums_ref[0:half, :], axis=0, keepdims=True)
    far = jnp.sum(sums_ref[half:, :], axis=0, keepdims=True)
    sums = jnp.where(section_ref[0] == 0, far, near)
    lane1 = lax.broadcasted_iota(I32, (1, LANES), 1)
    whole = jnp.sum(jnp.where(lane1 == fields, sums, 0.0), axis=1, keepdims=True)
    deficit = sums / whole
    mask = jnp.where(section_ref[0] == 0, 1.0, sea_ref[...].astype(F32))
    for f in range(fields):
        d = jnp.sum(jnp.where(lane1 == f, deficit, 0.0), axis=1, keepdims=True)
        out_ref[0, f] = masked_ref[f] + mask * d


VMEM = pl.BlockSpec(memory_space=pltpu.VMEM)
SMEM = pl.BlockSpec(memory_space=pltpu.SMEM)
HBM = pl.BlockSpec(memory_space=pltpu.HBM)


def shards(surface, area, sea, weights, src_row, dst_tile, dst_local):
    tiles = lax.axis_size("tile")
    section = lax.axis_index("comp").astype(I32).reshape(1)
    _, fields, rows, cells = surface.shape
    blocks = weights.shape[1]
    slots = 2 * blocks // tiles
    pitch = fields * slots + 1
    swap = [(0, 1), (1, 0)]
    up = [(i, i + 1) for i in range(tiles - 1)]
    down = [(i + 1, i) for i in range(tiles - 1)]

    before = lax.ppermute(surface[0, :, rows - 1], "tile", up)
    after = lax.ppermute(surface[0, :, 0], "tile", down)
    area_far = lax.ppermute(area, "comp", swap)
    code = (dst_tile[:, :, 0] << 14) | (dst_local << 7) | src_row

    sizes = dict(blocks=blocks, fields=fields, rows=rows, slots=slots, tiles=tiles)
    smooth, early, spot, targets = pl.pallas_call(
        functools.partial(prepare_kernel, **sizes),
        out_shape=(
            jax.ShapeDtypeStruct((rows * fields, LANES), F32),
            jax.ShapeDtypeStruct((blocks // CHUNKS, cells, cells), F32),
            jax.ShapeDtypeStruct((1, blocks), I32),
            jax.ShapeDtypeStruct((tiles, LANES), F32),
        ),
        in_specs=[VMEM, VMEM, HBM],
        out_specs=(VMEM,) * 4,
        scratch_shapes=[pltpu.SemaphoreType.DMA((EARLY,))],
        compiler_params=pltpu.CompilerParams(vmem_limit_bytes=46 << 20),
        cost_estimate=pl.CostEstimate(flops=10**7, bytes_accessed=8 << 20, transcendentals=0),
        name="prepare",
    )(code, surface, weights)

    packed, area_far, rim = pl.pallas_call(
        functools.partial(products_kernel, **sizes),
        out_shape=(
            jax.ShapeDtypeStruct((tiles * pitch, LANES), F32),
            jax.ShapeDtypeStruct((1, rows, cells), F32),
            jax.ShapeDtypeStruct((2, fields, LANES), F32),
        ),
        in_specs=[SMEM] * 2 + [VMEM] * 6 + [HBM],
        out_specs=(VMEM, VMEM, VMEM),
        scratch_shapes=[
            pltpu.VMEM((blocks - blocks // CHUNKS, cells, cells), F32),
            pltpu.VMEM((rows, 2 * SUB, cells), BF16),
            pltpu.SemaphoreType.DMA(((CHUNKS - 1) * PIECES,)),
        ],
        compiler_params=pltpu.CompilerParams(vmem_limit_bytes=46 << 20),
        cost_estimate=pl.CostEstimate(flops=2 * 10**8, bytes_accessed=20 << 20, transcendentals=0),
        name="products",
    )(section, spot, targets, smooth, before, after, area_far, early, weights)

    flat = packed.reshape(tiles, 1, pitch * LANES)
    recv = lax.all_to_all(flat, "tile", 0, 0, tiled=True).reshape(tiles * pitch, LANES)

    masked, tail = pl.pallas_call(
        functools.partial(place_kernel, fields=fields, rows=rows, slots=slots, tiles=tiles),
        out_shape=(
            jax.ShapeDtypeStruct((fields, rows, cells), F32),
            jax.ShapeDtypeStruct((2 * tiles, LANES), F32),
        ),
        in_specs=[SMEM] + [VMEM] * 6,
        out_specs=(VMEM, VMEM),
        compiler_params=pltpu.CompilerParams(vmem_limit_bytes=24 << 20),
        name="place",
    )(section, recv, smooth, rim, area, area_far, sea)

    masked = lax.ppermute(masked, "comp", swap)
    sums = lax.all_to_all(tail, ("comp", "tile"), 0, 0, tiled=True)

    return pl.pallas_call(
        functools.partial(correct_kernel, fields=fields),
        out_shape=jax.ShapeDtypeStruct((1, fields, rows, cells), F32),
        in_specs=[SMEM, VMEM, VMEM, VMEM],
        out_specs=VMEM,
        compiler_params=pltpu.CompilerParams(vmem_limit_bytes=16 << 20),
        name="correct",
    )(section, masked, sums, sea)


def solution(mesh):
    placed = (
        P("comp", None, "tile", None),
        P("comp", "tile", None),
        P("tile", None),
        P("comp", "tile", None, None),
        P("comp", "tile"),
        P("comp", "tile", None),
        P("comp", "tile"),
    )
    return jax.shard_map(
        shards, mesh=mesh, in_specs=placed, out_specs=P("comp", None, "tile", None), check_vma=False
    )
```

```python
import functools

import jax
import jax.numpy as jnp
from jax import lax
from jax.experimental import pallas as pl
from jax.experimental.pallas import tpu as pltpu
from jax.sharding import PartitionSpec as P

RATE = 0.2
LANES = 128
SUB = 8
CHUNKS = 8
PIECES = 2
EARLY = 4

F32 = jnp.float32
BF16 = jnp.bfloat16
I32 = jnp.int32


def split_rows(rows):
    lead = rows.astype(BF16).astype(F32)
    return jnp.concatenate([lead, rows - lead], axis=0).astype(BF16)


def block_product(rows2, w):
    lead = w.astype(BF16)
    rest = (w - lead.astype(F32)).astype(BF16)
    both = jnp.concatenate([lead, rest], axis=0)
    t = lax.dot_general(rows2, both, (((1,), (1,)), ((), ())), preferred_element_type=F32)
    t = t[:, :LANES] + t[:, LANES:]
    return t[:SUB] + t[SUB:]


def prepare_kernel(
    code_ref, surf_ref, w_hbm,
    smooth_ref, w_ref, spot_ref, targets_ref,
    sems, *, blocks, fields, rows, slots, tiles,
):
    size = w_ref.shape[0] // EARLY
    copies = [
        pltpu.make_async_copy(
            w_hbm.at[0, pl.ds(p * size, size)], w_ref.at[pl.ds(p * size, size)], sems.at[p]
        )
        for p in range(EARLY)
    ]
    for copy in copies:
        copy.start()
    r_iota = lax.broadcasted_iota(I32, (rows, LANES), 0)
    c_iota = lax.broadcasted_iota(I32, (rows, LANES), 1)
    for f in range(fields):
        s = surf_ref[0, f]
        n = jnp.where(r_iota > 0, pltpu.roll(s, 1, 0), 0.0)
        n += jnp.where(r_iota < rows - 1, pltpu.roll(s, rows - 1, 0), 0.0)
        n += jnp.where(c_iota > 0, pltpu.roll(s, 1, 1), 0.0)
        n += jnp.where(c_iota < LANES - 1, pltpu.roll(s, LANES - 1, 1), 0.0)
        sm = s + RATE * (n - 4.0 * s)
        smooth_ref[pl.ds(f, rows, stride=fields), :] = sm

    pitch = fields * slots + 1
    code = code_ref[...]
    tile = (code >> 14).astype(F32)
    local = ((code >> 7) & (rows - 1)).astype(F32)

    def column(v):
        parts = [v[:, i : i + LANES] for i in range(0, blocks, LANES)]
        return jnp.concatenate([jnp.broadcast_to(p, (LANES, LANES)).T for p in parts], axis=0)

    def ones(mask):
        return jnp.where(mask, 1.0, 0.0).astype(BF16)

    def count(a, b):
        return jnp.dot(a, b, preferred_element_type=F32)

    down = lax.broadcasted_iota(I32, (blocks, blocks), 0)
    right = lax.broadcasted_iota(I32, (blocks, blocks), 1)
    same = jnp.concatenate([column(tile)] * (blocks // LANES), axis=1) == tile
    rank = count(jnp.ones((SUB, blocks), BF16), ones(same & (down < right)))[0:1]
    rank_down = count(ones(same & (right < down)), jnp.ones((blocks, LANES), BF16))
    spot_ref[...] = ((code >> 14) * pitch + rank.astype(I32)) * rows + (code & (rows - 1))
    tiles_down = lax.broadcasted_iota(I32, (tiles, blocks), 0).astype(F32)
    lane = lax.broadcasted_iota(I32, (blocks, LANES), 1).astype(F32)
    value = jnp.where(lane == rank_down, column(local) + 1.0, 0.0).astype(BF16)
    targets_ref[...] = count(ones(tiles_down == tile), value) - 1.0

    for copy in copies:
        copy.wait()


def products_kernel(
    section_ref, spot_ref, targets_ref, smooth_ref, before_ref, after_ref, far_ref, early_ref,
    w_hbm,
    packed_ref, area_ref, rim_ref,
    wbuf, rows2, w_sems,
    *, blocks, fields, rows, slots, tiles,
):
    per = blocks // CHUNKS
    pitch = fields * slots + 1

    size = per // PIECES

    def fetch(p):
        return pltpu.make_async_copy(
            w_hbm.at[0, pl.ds(per + p * size, size)], wbuf.at[pl.ds(p * size, size)], w_sems.at[p]
        )

    for p in range((CHUNKS - 1) * PIECES):
        fetch(p).start()

    area_ref[...] = far_ref[...]
    before = RATE * before_ref[...]
    after = RATE * after_ref[...]
    rim_ref[0] = before
    rim_ref[1] = after

    packed_ref[pl.ds(fields * slots, tiles, stride=pitch), :] = targets_ref[...]

    def halves(g, carry):
        rows2[g] = split_rows(smooth_ref[pl.ds(pl.multiple_of(g * SUB, SUB), SUB), :])
        return carry

    lax.fori_loop(0, rows, halves, 0, unroll=8)
    rows2[0] = split_rows(smooth_ref[0:SUB, :] + before)
    rows2[rows - 1] = split_rows(smooth_ref[pl.ds((rows - 1) * SUB, SUB), :] + after)

    def chunk(c, w_ref):
        spots = [spot_ref[0, c * per + b] for b in range(per)]
        for b, spot in enumerate(spots):
            out = block_product(rows2[spot & (rows - 1)], w_ref[b])
            packed_ref[pl.ds(spot >> 7, SUB, stride=slots), :] = out

    def later(c, carry):
        for p in range(PIECES):
            fetch(c * PIECES + p).wait()
        chunk(c + 1, wbuf.at[pl.ds(c * per, per)])
        return carry

    chunk(0, early_ref)
    lax.fori_loop(0, CHUNKS - 1, later, 0)


def place_kernel(
    section_ref, recv_ref, smooth_ref, rim_ref, own_ref, area_ref, sea_ref, masked_ref, tail_ref,
    *, fields, rows, slots, tiles,
):
    pitch = fields * slots + 1
    targets = recv_ref[pl.ds(fields * slots, tiles, stride=pitch), :]
    lane = lax.broadcasted_iota(I32, (tiles, rows), 1).astype(F32)
    target = jnp.concatenate(
        [jnp.broadcast_to(targets[:, j : j + 1], (tiles, rows)) for j in range(slots)], axis=0
    )
    placing = jnp.where(target == jnp.concatenate([lane] * slots, axis=0), 1.0, 0.0).T.astype(BF16)
    used = target >= 0.0
    mask = jnp.where(section_ref[0] == 1, 1.0, sea_ref[...].astype(F32))
    weight = area_ref[0] * mask
    own = own_ref[0]
    gaps = []
    for f in range(fields):
        x = jnp.concatenate(
            [recv_ref[pl.ds(f * slots + j, tiles, stride=pitch), :] for j in range(slots)], axis=0
        )
        x = jnp.where(used, x, 0.0)
        lead = x.astype(BF16)
        rest = (x - lead.astype(F32)).astype(BF16)
        got = jnp.dot(placing, lead, preferred_element_type=F32)
        got += jnp.dot(placing, rest, preferred_element_type=F32)
        masked_ref[f] = got * mask
        source = own * smooth_ref[pl.ds(f, rows, stride=fields), :]
        edge = own[0:1] * rim_ref[0, f : f + 1] + own[rows - 1 : rows] * rim_ref[1, f : f + 1]
        gaps.append(jnp.sum(source - weight * got, axis=0, keepdims=True) + edge)
    gaps.append(jnp.sum(weight, axis=0, keepdims=True))
    gaps.append(jnp.zeros((2 * SUB - len(gaps), LANES), F32))
    sums = jnp.sum(jnp.concatenate(gaps, axis=0), axis=1, keepdims=True)
    down = lax.broadcasted_iota(I32, (2 * SUB, LANES), 0)
    right = lax.broadcasted_iota(I32, (2 * SUB, LANES), 1)
    tail = jnp.sum(jnp.where(down == right, sums, 0.0), axis=0, keepdims=True)
    tail_ref[...] = jnp.broadcast_to(tail, (2 * tiles, LANES))


def correct_kernel(section_ref, masked_ref, sums_ref, sea_ref, out_ref, *, fields):
    half = sums_ref.shape[0] // 2
    near = jnp.sum(sums_ref[0:half, :], axis=0, keepdims=True)
    far = jnp.sum(sums_ref[half:, :], axis=0, keepdims=True)
    sums = jnp.where(section_ref[0] == 0, far, near)
    lane1 = lax.broadcasted_iota(I32, (1, LANES), 1)
    whole = jnp.sum(jnp.where(lane1 == fields, sums, 0.0), axis=1, keepdims=True)
    deficit = sums / whole
    mask = jnp.where(section_ref[0] == 0, 1.0, sea_ref[...].astype(F32))
    for f in range(fields):
        d = jnp.sum(jnp.where(lane1 == f, deficit, 0.0), axis=1, keepdims=True)
        out_ref[0, f] = masked_ref[f] + mask * d


VMEM = pl.BlockSpec(memory_space=pltpu.VMEM)
SMEM = pl.BlockSpec(memory_space=pltpu.SMEM)
HBM = pl.BlockSpec(memory_space=pltpu.HBM)


def shards(surface, area, sea, weights, src_row, dst_tile, dst_local):
    tiles = lax.axis_size("tile")
    section = lax.axis_index("comp").astype(I32).reshape(1)
    _, fields, rows, cells = surface.shape
    blocks = weights.shape[1]
    slots = 2 * blocks // tiles
    pitch = fields * slots + 1
    swap = [(0, 1), (1, 0)]
    up = [(i, i + 1) for i in range(tiles - 1)]
    down = [(i + 1, i) for i in range(tiles - 1)]

    before = lax.ppermute(surface[0, :, rows - 1], "tile", up)
    after = lax.ppermute(surface[0, :, 0], "tile", down)
    area_far = lax.ppermute(area, "comp", swap)
    code = (dst_tile[:, :, 0] << 14) | (dst_local << 7) | src_row

    sizes = dict(blocks=blocks, fields=fields, rows=rows, slots=slots, tiles=tiles)
    smooth, early, spot, targets = pl.pallas_call(
        functools.partial(prepare_kernel, **sizes),
        out_shape=(
            jax.ShapeDtypeStruct((rows * fields, LANES), F32),
            jax.ShapeDtypeStruct((blocks // CHUNKS, cells, cells), F32),
            jax.ShapeDtypeStruct((1, blocks), I32),
            jax.ShapeDtypeStruct((tiles, LANES), F32),
        ),
        in_specs=[VMEM, VMEM, HBM],
        out_specs=(VMEM,) * 4,
        scratch_shapes=[pltpu.SemaphoreType.DMA((EARLY,))],
        compiler_params=pltpu.CompilerParams(vmem_limit_bytes=46 << 20),
        cost_estimate=pl.CostEstimate(flops=10**7, bytes_accessed=8 << 20, transcendentals=0),
        name="prepare",
    )(code, surface, weights)

    packed, area_far, rim = pl.pallas_call(
        functools.partial(products_kernel, **sizes),
        out_shape=(
            jax.ShapeDtypeStruct((tiles * pitch, LANES), F32),
            jax.ShapeDtypeStruct((1, rows, cells), F32),
            jax.ShapeDtypeStruct((2, fields, LANES), F32),
        ),
        in_specs=[SMEM] * 2 + [VMEM] * 6 + [HBM],
        out_specs=(VMEM, VMEM, VMEM),
        scratch_shapes=[
            pltpu.VMEM((blocks - blocks // CHUNKS, cells, cells), F32),
            pltpu.VMEM((rows, 2 * SUB, cells), BF16),
            pltpu.SemaphoreType.DMA(((CHUNKS - 1) * PIECES,)),
        ],
        compiler_params=pltpu.CompilerParams(vmem_limit_bytes=46 << 20),
        cost_estimate=pl.CostEstimate(flops=2 * 10**8, bytes_accessed=20 << 20, transcendentals=0),
        name="products",
    )(section, spot, targets, smooth, before, after, area_far, early, weights)

    flat = packed.reshape(tiles, 1, pitch * LANES)
    recv = lax.all_to_all(flat, "tile", 0, 0, tiled=True).reshape(tiles * pitch, LANES)

    masked, tail = pl.pallas_call(
        functools.partial(place_kernel, fields=fields, rows=rows, slots=slots, tiles=tiles),
        out_shape=(
            jax.ShapeDtypeStruct((fields, rows, cells), F32),
            jax.ShapeDtypeStruct((2 * tiles, LANES), F32),
        ),
        in_specs=[SMEM] + [VMEM] * 6,
        out_specs=(VMEM, VMEM),
        compiler_params=pltpu.CompilerParams(vmem_limit_bytes=24 << 20),
        name="place",
    )(section, recv, smooth, rim, area, area_far, sea)

    masked = lax.ppermute(masked, "comp", swap)
    sums = lax.all_to_all(tail, ("comp", "tile"), 0, 0, tiled=True)

    return pl.pallas_call(
        functools.partial(correct_kernel, fields=fields),
        out_shape=jax.ShapeDtypeStruct((1, fields, rows, cells), F32),
        in_specs=[SMEM, VMEM, VMEM, VMEM],
        out_specs=VMEM,
        compiler_params=pltpu.CompilerParams(vmem_limit_bytes=16 << 20),
        name="correct",
    )(section, masked, sums, sea)


def solution(mesh):
    placed = (
        P("comp", None, "tile", None),
        P("comp", "tile", None),
        P("tile", None),
        P("comp", "tile", None, None),
        P("comp", "tile"),
        P("comp", "tile", None),
        P("comp", "tile"),
    )
    return jax.shard_map(
        shards, mesh=mesh, in_specs=placed, out_specs=P("comp", None, "tile", None), check_vma=False
    )
```
